32 devices in a mesh: row: 8 (over z, x), chan: 4 (over y, core).
Axes of the slice: x: 2, y: 2, z: 4, core: 2. Of those that a mesh axis runs over, the one named last changes fastest.
Arguments:
- image: bfloat16 [32, 4096, 4096], P('chan', 'row'), may hold values from -6 to 6
- spec_weight: bfloat16 [2, 256, 32, 32, 256], P(None, 'row', None, 'chan'), may hold values from -0.75 to 0.75
- point_weight: bfloat16 [32, 32], replicated, may hold values from -1 to 1
- bias: float32 [32], P('chan'), may hold values from -3 to 3
Outputs:
- layer_out: bfloat16 [32, 4096, 4096], P('chan', 'row')
The draws below stay inside these ranges and needn't reach their ends.
All inputs are finite; a program needn't handle non-finite values.
Results may differ from the reference program's by a relative error of at most 0.012.
Values may be sent and summed in bfloat16 or wider, within the bound.
A program may use at most 384 MiB of HBM per device.

```python
import math
import jax
import jax.numpy as jnp
from jax import lax

C = 32
H = 4096
W = 4096
MX = 256
MY = 256


def levels(key, shape, pieces, least, largest):
    factor_of = 1.0
    for dim, parts in pieces:
        steps = jax.random.uniform(jax.random.fold_in(jax.random.fold_in(key, 6), dim), (parts,), jnp.float32, least / len(pieces), largest / len(pieces))
        factor_of = factor_of * jnp.repeat(jnp.exp(steps), shape[dim] // parts).reshape((-1,) + (1,) * (len(shape) - 1 - dim))
    return factor_of


def centred(rng, shape, spread, bound, split=(), kind=jnp.bfloat16):
    level = levels(rng, shape, split, -0.22, 0.18) if split else 1.0
    result = jax.random.normal(rng, shape, jnp.float32) * spread * level
    return jnp.minimum(jnp.maximum(result, -bound), bound).astype(kind)


def setup_inputs(seed: int = 0) -> dict:
    streams_of = jax.random.split(jax.random.key(seed), 5)
    image = centred(streams_of[0], (C, H, W), 1.0, 6.0, ((0, 4), (1, 8)))
    spec_weight = centred(streams_of[1], (2, MX, C, C, MY), (2 * C) ** -0.5, 0.75, ((1, 8), (3, 4)))
    point_weight = centred(streams_of[2], (C, C), C ** -0.5, 1.0)
    bias = centred(streams_of[3], (C,), 0.5, 3.0, ((0, 4),), jnp.float32)
    return {"image": image, "spec_weight": spec_weight, "point_weight": point_weight, "bias": bias}


def wave_table(points, freqs, length):
    prod = jnp.mod(points[:, None] * freqs[None, :], length)
    angle = prod.astype(jnp.float32) * (2.0 * math.pi / length)
    return (jnp.cos(angle), jnp.sin(angle))

def reference(image, spec_weight, point_weight, bias):
    col_pts = jnp.arange(W, dtype=jnp.int32)
    col_freq = jnp.arange(MY, dtype=jnp.int32)
    cos_w, sin_w = wave_table(col_pts, col_freq, W)
    fwd_cols = jnp.concatenate([cos_w, -sin_w], 1).astype(jnp.bfloat16)
    back_cols = jnp.concatenate([cos_w.T, -sin_w.T], 0).astype(jnp.bfloat16)
    row_pts = jnp.arange(H, dtype=jnp.int32)
    row_freq = jnp.arange(MX, dtype=jnp.int32) - MX // 2
    cos_h, sin_h = wave_table(row_pts, row_freq, H)
    fwd_rows = jnp.concatenate([cos_h, sin_h], 1).T.astype(jnp.bfloat16)

    def forward(plane):
        colspec = (jnp.dot(plane, fwd_cols, preferred_element_type=jnp.float32) * (1.0 / math.sqrt(W))).astype(jnp.bfloat16)
        partial_value = jnp.dot(fwd_rows, colspec, preferred_element_type=jnp.float32)
        spec_re = partial_value[:MX, :MY] + partial_value[MX:, MY:]
        spec_im = partial_value[:MX, MY:] - partial_value[MX:, :MY]
        return (jnp.concatenate([spec_re, spec_im], 1) * (1.0 / math.sqrt(H))).astype(jnp.bfloat16)
    spectrum = lax.map(forward, image)
    zed_re = spectrum[..., :MY].astype(jnp.float32)
    zed_im = spectrum[..., MY:].astype(jnp.float32)
    wgt_re = spec_weight[0].astype(jnp.float32)
    wgt_im = spec_weight[1].astype(jnp.float32)
    mix_re = jnp.einsum('kiop,ikp->okp', wgt_re, zed_re) - jnp.einsum('kiop,ikp->okp', wgt_im, zed_im)
    mix_im = jnp.einsum('kiop,ikp->okp', wgt_re, zed_im) + jnp.einsum('kiop,ikp->okp', wgt_im, zed_re)
    mixed = jnp.concatenate([mix_re, mix_im], -1).astype(jnp.bfloat16).astype(jnp.float32)
    cos_back = cos_h.T.astype(jnp.bfloat16).astype(jnp.float32)
    sin_back = sin_h.T.astype(jnp.bfloat16).astype(jnp.float32)
    with_cos = jnp.einsum('okp,kh->ohp', mixed, cos_back)
    with_sin = jnp.einsum('okp,kh->ohp', mixed, sin_back)
    back_re = with_cos[..., :MY] - with_sin[..., MY:]
    back_im = with_sin[..., :MY] + with_cos[..., MY:]
    rowback = (jnp.concatenate([back_re, back_im], -1) * (1.0 / math.sqrt(MX))).astype(jnp.bfloat16)
    flat_image = image.reshape(C, H * W)

    def out_channel(channel):
        spectral = jnp.dot(rowback[channel], back_cols, preferred_element_type=jnp.float32) * (1.0 / math.sqrt(MY))
        weight_row = lax.dynamic_slice_in_dim(point_weight, channel, 1, 0)
        pointwise = jnp.dot(weight_row, flat_image, preferred_element_type=jnp.float32).reshape(H, W).astype(jnp.bfloat16)
        total = spectral + pointwise.astype(jnp.float32) + bias[channel]
        return jax.nn.gelu(total, approximate=False).astype(jnp.bfloat16)
    return lax.map(out_channel, jnp.arange(C, dtype=jnp.int32))
```

```python
import math

import jax
import jax.numpy as jnp
from jax import lax
from jax.experimental import pallas as pl
from jax.experimental.pallas import tpu as pltpu
from jax.sharding import PartitionSpec as P

MX = 256
MY = 256
UNIT = 16
SLACK = 5


def wave_table(points, freqs, length):
    prod = jnp.mod(points[:, None] * freqs[None, :], length)
    angle = prod.astype(jnp.float32) * (2.0 * math.pi / length)
    return (jnp.cos(angle), jnp.sin(angle))


def chunk_rows(row_count):
    if row_count >= 512:
        middle, rest = divmod(row_count - 128, 64)
        sizes = [32] + [64] * middle + [48, 32, 16] + [UNIT] * (rest // UNIT)
    else:
        sizes = [UNIT] * (row_count // UNIT)
    starts = [sum(sizes[:n]) for n in range(len(sizes))]
    return list(zip(starts, sizes))


def partial_kernel(one_ref, two_ref, kron_ref, *out_refs):
    chans, rows, width = one_ref.shape
    half = chans * rows
    tile = 1024

    @pl.loop(0, width // tile)
    def _(step):
        cols = pl.ds(pl.multiple_of(step * tile, tile), tile)
        both = jnp.concatenate(
            [one_ref[:, :, cols].reshape(half, tile), two_ref[:, :, cols].reshape(half, tile)], 0
        )
        part = jnp.dot(kron_ref[...], both, preferred_element_type=jnp.float32)
        part = part.astype(jnp.bfloat16)
        for n, out_ref in enumerate(out_refs):
            out_ref[:, :, cols] = part[n * half : (n + 1) * half].reshape(chans, rows, tile)


def partials(one, two, kron, start, rows):
    chans, _, width = one.shape
    first = start // UNIT
    block = (chans, UNIT, width)
    count = kron.shape[0] // (chans * UNIT)
    shape = jax.ShapeDtypeStruct((chans, rows, width), jnp.bfloat16)
    return pl.pallas_call(
        partial_kernel,
        grid=(rows // UNIT,),
        in_specs=[
            pl.BlockSpec(block, lambda t: (0, first + t, 0)),
            pl.BlockSpec(block, lambda t: (0, t, 0)),
            pl.BlockSpec(kron.shape, lambda t: (0, 0)),
        ],
        out_specs=[pl.BlockSpec(block, lambda t: (0, t, 0))] * count,
        out_shape=[shape] * count,
        compiler_params=pltpu.CompilerParams(vmem_limit_bytes=32 << 20),
        cost_estimate=pl.CostEstimate(
            flops=2 * count * chans * rows * width * kron.shape[1],
            bytes_accessed=(2 + count) * chans * rows * width * 2,
            transcendentals=0,
        ),
    )(one, two, kron)


def final_kernel(bias_ref, back_ref, cols_ref, home_ref, came_ref, *rest):
    out_ref = rest[-1]
    chans, rows, width = home_ref.shape
    tile = 512
    flat = back_ref[...].reshape(chans * rows, back_ref.shape[2])
    bias = bias_ref[...].reshape(chans, 1, 1)

    @pl.loop(0, width // tile)
    def _(step):
        cols = pl.ds(pl.multiple_of(step * tile, tile), tile)
        spectral = jnp.dot(flat, cols_ref[:, cols], preferred_element_type=jnp.float32)
        total = spectral.reshape(chans, rows, tile) + bias
        total += home_ref[:, :, cols].astype(jnp.float32)
        total += came_ref[:, :, cols].astype(jnp.float32)
        value = 0.5 * total * (1.0 + lax.erf(total * math.sqrt(0.5)))
        out_ref[:, :, cols] = value.astype(jnp.bfloat16)


def finish(bias, rowback, back_cols, home, came, start, held):
    chans, rows, width = home.shape
    row_count = rowback.shape[1]
    tall = 32 if rows % 32 == 0 and start % 32 == 0 else UNIT
    first = start // tall
    block = (chans, tall, width)
    in_specs = [
        pl.BlockSpec((chans, 1), lambda t: (0, 0)),
        pl.BlockSpec((chans, tall, 2 * MY), lambda t: (0, first + t, 0)),
        pl.BlockSpec(back_cols.shape, lambda t: (0, 0)),
        pl.BlockSpec(block, lambda t: (0, t, 0)),
        pl.BlockSpec(block, lambda t: (0, t, 0)),
    ]
    operands = [bias, rowback, back_cols, home, came]
    aliases = {}
    if held is not None:
        in_specs.append(pl.BlockSpec(memory_space=pl.ANY))
        operands.append(held)
        aliases = {5: 0}
    size = chans * rows * width
    return pl.pallas_call(
        final_kernel,
        grid=(rows // tall,),
        in_specs=in_specs,
        out_specs=pl.BlockSpec(block, lambda t: (0, first + t, 0)),
        out_shape=jax.ShapeDtypeStruct((chans, row_count, width), jnp.bfloat16),
        input_output_aliases=aliases,
        compiler_params=pltpu.CompilerParams(vmem_limit_bytes=48 << 20),
        cost_estimate=pl.CostEstimate(
            flops=2 * size * 2 * MY, bytes_accessed=3 * size * 2, transcendentals=size
        ),
    )(*operands)


def on_device(image, spec_weight, point_weight, bias):
    chan_count, row_count, width_len = image.shape
    row_index = lax.axis_index("row")
    row_devs = lax.axis_size("row")
    chan_devs = lax.axis_size("chan")
    chan_index = lax.axis_index("chan")
    full_rows = row_count * row_devs

    core_swap = [(c, c ^ 1) for c in range(chan_devs)]
    chip_swap = [(c, c ^ 2) for c in range(chan_devs)]
    chunks = chunk_rows(row_count)
    first_mine = lax.slice_in_dim(image, 0, chunks[0][1], axis=1)
    first_far = lax.ppermute(first_mine, "chan", chip_swap)
    first_mine, image = lax.optimization_barrier((first_mine, image))
    peers = [lax.ppermute(first_mine, "chan", core_swap)]
    for start, rows in chunks[1:]:
        mine = lax.slice_in_dim(image, start, start + rows, axis=1)
        peers.append(lax.ppermute(mine, "chan", core_swap))

    def kron(out_dev, in_dev):
        eye = jnp.eye(UNIT, dtype=jnp.bfloat16)
        blocks = [
            lax.dynamic_slice(
                point_weight, (out_dev * chan_count, dev * chan_count), (chan_count, chan_count)
            )
            for dev in (in_dev, in_dev ^ 1)
        ]
        small = jnp.concatenate(blocks, 1)
        large = small[:, None, :, None] * eye[None, :, None, :]
        return large.reshape(chan_count * UNIT, 2 * chan_count * UNIT)

    kron_home = kron(chan_index, chan_index)
    kron_far = kron(chan_index, chan_index ^ 2)
    kron_both = jnp.concatenate([kron(chan_index ^ 2, chan_index), kron_home], 0)

    row_global = row_index * row_count + jnp.arange(row_count, dtype=jnp.int32)
    col_pts = jnp.arange(width_len, dtype=jnp.int32)
    col_freq = jnp.arange(MY, dtype=jnp.int32)
    cos_w, sin_w = wave_table(col_pts, col_freq, width_len)
    fwd_cols = jnp.concatenate([cos_w, -sin_w], 1).astype(jnp.bfloat16)
    back_cols = jnp.concatenate([cos_w.T, -sin_w.T], 0).astype(jnp.bfloat16)
    back_cols = back_cols * jnp.bfloat16(1.0 / math.sqrt(MY))
    row_freq = jnp.arange(MX, dtype=jnp.int32) - MX // 2
    colspec = jnp.dot(
        image.reshape(chan_count * row_count, width_len),
        fwd_cols,
        preferred_element_type=jnp.float32,
    )
    colspec = (
        (colspec * (1.0 / math.sqrt(width_len)))
        .astype(jnp.bfloat16)
        .reshape(chan_count, row_count, 2 * MY)
    )
    cos_h, sin_h = wave_table(row_global, row_freq, full_rows)
    fwd_rows = jnp.concatenate([cos_h, sin_h], 1).astype(jnp.bfloat16)
    partial_value = jnp.einsum("chp,hq->cqp", colspec, fwd_rows, preferred_element_type=jnp.float32)
    spec_re = partial_value[:, :MX, :MY] + partial_value[:, MX:, MY:]
    spec_im = partial_value[:, :MX, MY:] - partial_value[:, MX:, :MY]
    partial_value = jnp.concatenate([spec_re, spec_im], -1) * (1.0 / math.sqrt(full_rows))
    block = lax.psum_scatter(partial_value, "row", scatter_dimension=1, tiled=True)
    spectrum = block.astype(jnp.bfloat16)
    all_inputs = lax.all_gather(spectrum, "chan", axis=0, tiled=True)
    zed_re = all_inputs[..., :MY].astype(jnp.float32)
    zed_im = all_inputs[..., MY:].astype(jnp.float32)
    wgt_re = spec_weight[0].astype(jnp.float32)
    wgt_im = spec_weight[1].astype(jnp.float32)
    mix_re = jnp.einsum("kiop,ikp->okp", wgt_re, zed_re) - jnp.einsum(
        "kiop,ikp->okp", wgt_im, zed_im
    )
    mix_im = jnp.einsum("kiop,ikp->okp", wgt_re, zed_im) + jnp.einsum(
        "kiop,ikp->okp", wgt_im, zed_re
    )
    mixed = jnp.concatenate([mix_re, mix_im], -1).astype(jnp.bfloat16)
    piece = lax.all_gather(mixed, "row", axis=1, tiled=True)
    cos_back = cos_h.T.astype(jnp.bfloat16)
    sin_back = sin_h.T.astype(jnp.bfloat16)
    with_cos = jnp.einsum("okp,kh->ohp", piece, cos_back, preferred_element_type=jnp.float32)
    with_sin = jnp.einsum("okp,kh->ohp", piece, sin_back, preferred_element_type=jnp.float32)
    back_re = with_cos[..., :MY] - with_sin[..., MY:]
    back_im = with_sin[..., :MY] + with_cos[..., MY:]
    rowback = (jnp.concatenate([back_re, back_im], -1) * (1.0 / math.sqrt(MX))).astype(jnp.bfloat16)

    bias = bias[:, None]
    held = None
    homes, cames = [], []
    done = 0

    def finish_next():
        return finish(bias, rowback, back_cols, homes[done], cames[done], chunks[done][0], held)

    for n, (start, rows) in enumerate(chunks):
        if n == 0:
            first_other = lax.ppermute(first_far, "chan", core_swap)
            homes += partials(image, peers[0], kron_home, start, rows)
            cames += partials(first_far, first_other, kron_far, 0, rows)
            continue
        away, home = partials(image, peers[n], kron_both, start, rows)
        if n >= 2:
            before = first_far if n == 2 else cames[n - 2]
            away, before = lax.optimization_barrier((away, before))
            if n > 2:
                cames[n - 2] = before
        if n >= SLACK:
            while done <= n - 3:
                held = finish_next()
                done += 1
            away, held = lax.optimization_barrier((away, held))
        homes.append(home)
        cames.append(lax.ppermute(away, "chan", chip_swap))
    while done < len(chunks):
        held = finish_next()
        done += 1
    return held


def solution(mesh):
    in_specs = (P("chan", "row", None), P(None, "row", None, "chan", None), P(), P("chan"))
    out_specs = P("chan", "row", None)
    return jax.shard_map(
        on_device, mesh=mesh, in_specs=in_specs, out_specs=out_specs, check_vma=False
    )
```

```python
import math

import jax
import jax.numpy as jnp
from jax import lax
from jax.experimental import pallas as pl
from jax.experimental.pallas import tpu as pltpu
from jax.sharding import PartitionSpec as P

MX = 256
MY = 256
UNIT = 16
SLACK = 9


def wave_table(points, freqs, length):
    prod = jnp.mod(points[:, None] * freqs[None, :], length)
    angle = prod.astype(jnp.float32) * (2.0 * math.pi / length)
    return (jnp.cos(angle), jnp.sin(angle))


def chunk_rows(row_count):
    if row_count >= 256:
        middle, rest = divmod(row_count - 192, 64)
        sizes = [32, 32, 32] + [64] * middle + [48, 32, 16] + [UNIT] * (rest // UNIT)
    else:
        sizes = [UNIT] * (row_count // UNIT)
    starts = [sum(sizes[:n]) for n in range(len(sizes))]
    return list(zip(starts, sizes))


def partial_kernel(one_ref, two_ref, kron_ref, *out_refs):
    chans, rows, width = one_ref.shape
    half = chans * rows
    tile = 1024

    @pl.loop(0, width // tile)
    def _(step):
        cols = pl.ds(pl.multiple_of(step * tile, tile), tile)
        both = jnp.concatenate(
            [one_ref[:, :, cols].reshape(half, tile), two_ref[:, :, cols].reshape(half, tile)], 0
        )
        part = jnp.dot(kron_ref[...], both, preferred_element_type=jnp.float32)
        part = part.astype(jnp.bfloat16)
        for n, out_ref in enumerate(out_refs):
            out_ref[:, :, cols] = part[n * half : (n + 1) * half].reshape(chans, rows, tile)


def partials(one, two, kron, start, rows):
    chans, _, width = one.shape
    first = start // UNIT
    block = (chans, UNIT, width)
    count = kron.shape[0] // (chans * UNIT)
    shape = jax.ShapeDtypeStruct((chans, rows, width), jnp.bfloat16)
    return pl.pallas_call(
        partial_kernel,
        grid=(rows // UNIT,),
        in_specs=[
            pl.BlockSpec(block, lambda t: (0, first + t, 0)),
            pl.BlockSpec(block, lambda t: (0, t, 0)),
            pl.BlockSpec(kron.shape, lambda t: (0, 0)),
        ],
        out_specs=[pl.BlockSpec(block, lambda t: (0, t, 0))] * count,
        out_shape=[shape] * count,
        compiler_params=pltpu.CompilerParams(vmem_limit_bytes=32 << 20),
        cost_estimate=pl.CostEstimate(
            flops=2 * count * chans * rows * width * kron.shape[1],
            bytes_accessed=(2 + count) * chans * rows * width * 2,
            transcendentals=0,
        ),
    )(one, two, kron)


def final_kernel(bias_ref, back_ref, cols_ref, home_ref, came_ref, *rest):
    out_ref = rest[-1]
    chans, rows, width = home_ref.shape
    tile = 512
    flat = back_ref[...].reshape(chans * rows, back_ref.shape[2])
    bias = bias_ref[...].reshape(chans, 1, 1)

    @pl.loop(0, width // tile)
    def _(step):
        cols = pl.ds(pl.multiple_of(step * tile, tile), tile)
        spectral = jnp.dot(flat, cols_ref[:, cols], preferred_element_type=jnp.float32)
        total = spectral.reshape(chans, rows, tile) + bias
        total += home_ref[:, :, cols].astype(jnp.float32)
        total += came_ref[:, :, cols].astype(jnp.float32)
        value = 0.5 * total * (1.0 + lax.erf(total * math.sqrt(0.5)))
        out_ref[:, :, cols] = value.astype(jnp.bfloat16)


def finish(bias, rowback, back_cols, home, came, start, held):
    chans, rows, width = home.shape
    row_count = rowback.shape[1]
    tall = 32 if rows % 32 == 0 and start % 32 == 0 else UNIT
    first = start // tall
    block = (chans, tall, width)
    in_specs = [
        pl.BlockSpec((chans, 1), lambda t: (0, 0)),
        pl.BlockSpec((chans, tall, 2 * MY), lambda t: (0, first + t, 0)),
        pl.BlockSpec(back_cols.shape, lambda t: (0, 0)),
        pl.BlockSpec(block, lambda t: (0, t, 0)),
        pl.BlockSpec(block, lambda t: (0, t, 0)),
    ]
    operands = [bias, rowback, back_cols, home, came]
    aliases = {}
    if held is not None:
        in_specs.append(pl.BlockSpec(memory_space=pl.ANY))
        operands.append(held)
        aliases = {5: 0}
    size = chans * rows * width
    return pl.pallas_call(
        final_kernel,
        grid=(rows // tall,),
        in_specs=in_specs,
        out_specs=pl.BlockSpec(block, lambda t: (0, first + t, 0)),
        out_shape=jax.ShapeDtypeStruct((chans, row_count, width), jnp.bfloat16),
        input_output_aliases=aliases,
        compiler_params=pltpu.CompilerParams(vmem_limit_bytes=48 << 20),
        cost_estimate=pl.CostEstimate(
            flops=2 * size * 2 * MY, bytes_accessed=3 * size * 2, transcendentals=size
        ),
    )(*operands)


def on_device(image, spec_weight, point_weight, bias):
    chan_count, row_count, width_len = image.shape
    row_index = lax.axis_index("row")
    row_devs = lax.axis_size("row")
    chan_devs = lax.axis_size("chan")
    chan_index = lax.axis_index("chan")
    full_rows = row_count * row_devs

    core_swap = [(c, c ^ 1) for c in range(chan_devs)]
    chip_swap = [(c, c ^ 2) for c in range(chan_devs)]
    chunks = chunk_rows(row_count)
    def swap(part, start, rows):
        mine = lax.slice_in_dim(part, start, start + rows, axis=1)
        return lax.ppermute(mine, "chan", core_swap)

    first_mine = lax.slice_in_dim(image, 0, chunks[0][1], axis=1)
    first_far = lax.ppermute(first_mine, "chan", chip_swap)
    first_mine, image = lax.optimization_barrier((first_mine, image))

    def kron(out_dev, in_dev):
        eye = jnp.eye(UNIT, dtype=jnp.bfloat16)
        blocks = [
            lax.dynamic_slice(
                point_weight, (out_dev * chan_count, dev * chan_count), (chan_count, chan_count)
            )
            for dev in (in_dev, in_dev ^ 1)
        ]
        small = jnp.concatenate(blocks, 1)
        large = small[:, None, :, None] * eye[None, :, None, :]
        return large.reshape(chan_count * UNIT, 2 * chan_count * UNIT)

    kron_home = kron(chan_index, chan_index)
    kron_far = kron(chan_index, chan_index ^ 2)
    kron_both = jnp.concatenate([kron(chan_index ^ 2, chan_index), kron_home], 0)

    cames = {}
    homes = {}
    done = []

    peers = {}

    def meet(n):
        if n < len(chunks):
            peers[n] = swap(image, *chunks[n])

    def issue(n):
        if n >= len(chunks):
            return
        peer = peers[n]
        away, homes[n] = partials(image, peer, kron_both, *chunks[n])
        before = 3 * (n - SLACK) + 4
        if n >= SLACK:
            finish_until(before)
            away, done[before - 1] = lax.optimization_barrier((away, done[before - 1]))
        cames[n] = lax.ppermute(away, "chan", chip_swap)

    def gate(n, *values):
        if n + 1 >= len(chunks):
            return values
        cames[n], homes[n + 1], *values = lax.optimization_barrier(
            (cames[n], homes[n + 1], *values)
        )
        return values

    def finish_until(count):
        while len(done) < count:
            n = len(done)
            last = done[-1] if done else None
            done.append(
                finish(bias, rowback, back_cols, homes[n], cames[n], chunks[n][0], last)
            )

    meet(1)
    meet(2)
    issue(1)
    issue(2)
    col_pts = jnp.arange(width_len, dtype=jnp.int32)
    row_global = row_index * row_count + jnp.arange(row_count, dtype=jnp.int32)
    bias = bias[:, None]
    first_far, first_mine, image, col_pts = gate(1, first_far, first_mine, image, col_pts)
    meet(3)
    meet(4)
    issue(3)
    image, row_global = gate(2, image, row_global)

    col_freq = jnp.arange(MY, dtype=jnp.int32)
    cos_w, sin_w = wave_table(col_pts, col_freq, width_len)
    fwd_cols = jnp.concatenate([cos_w, -sin_w], 1).astype(jnp.bfloat16)
    back_cols = jnp.concatenate([cos_w.T, -sin_w.T], 0).astype(jnp.bfloat16)
    back_cols = back_cols * jnp.bfloat16(1.0 / math.sqrt(MY))
    row_freq = jnp.arange(MX, dtype=jnp.int32) - MX // 2
    colspec = jnp.dot(
        image.reshape(chan_count * row_count, width_len),
        fwd_cols,
        preferred_element_type=jnp.float32,
    )
    colspec = (
        (colspec * (1.0 / math.sqrt(width_len)))
        .astype(jnp.bfloat16)
        .reshape(chan_count, row_count, 2 * MY)
    )
    meet(5)
    issue(4)
    image, colspec = gate(3, image, colspec)
    meet(6)
    issue(5)
    cos_h, sin_h = wave_table(row_global, row_freq, full_rows)
    fwd_rows = jnp.concatenate([cos_h, sin_h], 1).astype(jnp.bfloat16)
    partial_value = jnp.einsum("chp,hq->cqp", colspec, fwd_rows, preferred_element_type=jnp.float32)
    spec_re = partial_value[:, :MX, :MY] + partial_value[:, MX:, MY:]
    spec_im = partial_value[:, :MX, MY:] - partial_value[:, MX:, :MY]
    partial_value = jnp.concatenate([spec_re, spec_im], -1) * (1.0 / math.sqrt(full_rows))
    block = lax.psum_scatter(partial_value, "row", scatter_dimension=1, tiled=True)
    (image,) = gate(4, image)
    meet(7)
    issue(6)
    image, block = gate(5, image, block)
    meet(8)
    issue(7)
    spectrum = block.astype(jnp.bfloat16)
    all_inputs = lax.all_gather(spectrum, "chan", axis=0, tiled=True)
    zed_re = all_inputs[..., :MY].astype(jnp.float32)
    zed_im = all_inputs[..., MY:].astype(jnp.float32)
    wgt_re = spec_weight[0].astype(jnp.float32)
    wgt_im = spec_weight[1].astype(jnp.float32)
    mix_re = jnp.einsum("kiop,ikp->okp", wgt_re, zed_re) - jnp.einsum(
        "kiop,ikp->okp", wgt_im, zed_im
    )
    mix_im = jnp.einsum("kiop,ikp->okp", wgt_re, zed_im) + jnp.einsum(
        "kiop,ikp->okp", wgt_im, zed_re
    )
    mixed = jnp.concatenate([mix_re, mix_im], -1).astype(jnp.bfloat16)
    piece = lax.all_gather(mixed, "row", axis=1, tiled=True)
    image, piece = gate(6, image, piece)
    meet(9)
    issue(8)
    cos_back = cos_h.T.astype(jnp.bfloat16)
    sin_back = sin_h.T.astype(jnp.bfloat16)
    with_cos = jnp.einsum("okp,kh->ohp", piece, cos_back, preferred_element_type=jnp.float32)
    with_sin = jnp.einsum("okp,kh->ohp", piece, sin_back, preferred_element_type=jnp.float32)
    back_re = with_cos[..., :MY] - with_sin[..., MY:]
    back_im = with_sin[..., :MY] + with_cos[..., MY:]
    rowback = (jnp.concatenate([back_re, back_im], -1) * (1.0 / math.sqrt(MX))).astype(jnp.bfloat16)

    first_peer = lax.ppermute(first_mine, "chan", core_swap)
    (homes[0],) = partials(image, first_peer, kron_home, *chunks[0])
    first_other = lax.ppermute(first_far, "chan", core_swap)
    (cames[0],) = partials(first_far, first_other, kron_far, 0, chunks[0][1])
    for n in range(9, len(chunks)):
        (image,) = gate(n - 2, image)
        meet(n + 1)
        issue(n)
    finish_until(len(chunks))
    return done[-1]


def solution(mesh):
    in_specs = (P("chan", "row", None), P(None, "row", None, "chan", None), P(), P("chan"))
    out_specs = P("chan", "row", None)
    return jax.shard_map(
        on_device, mesh=mesh, in_specs=in_specs, out_specs=out_specs, check_vma=False
    )
```

```python
import math

import jax
import jax.numpy as jnp
from jax import lax
from jax.experimental import pallas as pl
from jax.experimental.pallas import tpu as pltpu
from jax.sharding import PartitionSpec as P

MX = 256
MY = 256
UNIT = 16
SLACK = 9


def wave_table(points, freqs, length):
    prod = jnp.mod(points[:, None] * freqs[None, :], length)
    angle = prod.astype(jnp.float32) * (2.0 * math.pi / length)
    return (jnp.cos(angle), jnp.sin(angle))


def chunk_rows(row_count):
    if row_count >= 256:
        middle, rest = divmod(row_count - 192, 64)
        sizes = [32, 32, 32] + [64] * middle + [48, 32, 16] + [UNIT] * (rest // UNIT)
    else:
        sizes = [UNIT] * (row_count // UNIT)
    starts = [sum(sizes[:n]) for n in range(len(sizes))]
    return list(zip(starts, sizes))


def partial_kernel(one_ref, two_ref, kron_ref, *out_refs):
    chans, rows, width = one_ref.shape
    half = chans * rows
    tile = 1024

    @pl.loop(0, width // tile)
    def _(step):
        cols = pl.ds(pl.multiple_of(step * tile, tile), tile)
        both = jnp.concatenate(
            [one_ref[:, :, cols].reshape(half, tile), two_ref[:, :, cols].reshape(half, tile)], 0
        )
        part = jnp.dot(kron_ref[...], both, preferred_element_type=jnp.float32)
        part = part.astype(jnp.bfloat16)
        for n, out_ref in enumerate(out_refs):
            out_ref[:, :, cols] = part[n * half : (n + 1) * half].reshape(chans, rows, tile)


def partials(one, two, kron, start, rows):
    chans, _, width = one.shape
    first = start // UNIT
    block = (chans, UNIT, width)
    count = kron.shape[0] // (chans * UNIT)
    shape = jax.ShapeDtypeStruct((chans, rows, width), jnp.bfloat16)
    return pl.pallas_call(
        partial_kernel,
        grid=(rows // UNIT,),
        in_specs=[
            pl.BlockSpec(block, lambda t: (0, first + t, 0)),
            pl.BlockSpec(block, lambda t: (0, t, 0)),
            pl.BlockSpec(kron.shape, lambda t: (0, 0)),
        ],
        out_specs=[pl.BlockSpec(block, lambda t: (0, t, 0))] * count,
        out_shape=[shape] * count,
        compiler_params=pltpu.CompilerParams(vmem_limit_bytes=32 << 20),
        cost_estimate=pl.CostEstimate(
            flops=2 * count * chans * rows * width * kron.shape[1],
            bytes_accessed=(2 + count) * chans * rows * width * 2,
            transcendentals=0,
        ),
    )(one, two, kron)


def final_kernel(bias_ref, back_ref, cols_ref, home_ref, came_ref, *rest):
    out_ref = rest[-1]
    chans, rows, width = home_ref.shape
    tile = 512
    flat = back_ref[...].reshape(chans * rows, back_ref.shape[2])
    bias = bias_ref[...].reshape(chans, 1, 1)

    @pl.loop(0, width // tile)
    def _(step):
        cols = pl.ds(pl.multiple_of(step * tile, tile), tile)
        spectral = jnp.dot(flat, cols_ref[:, cols], preferred_element_type=jnp.float32)
        total = spectral.reshape(chans, rows, tile) + bias
        total += home_ref[:, :, cols].astype(jnp.float32)
        total += came_ref[:, :, cols].astype(jnp.float32)
        value = 0.5 * total * (1.0 + lax.erf(total * math.sqrt(0.5)))
        out_ref[:, :, cols] = value.astype(jnp.bfloat16)


def finish(bias, rowback, back_cols, home, came, start, held):
    chans, rows, width = home.shape
    row_count = rowback.shape[1]
    tall = 32 if rows % 32 == 0 and start % 32 == 0 else UNIT
    first = start // tall
    block = (chans, tall, width)
    in_specs = [
        pl.BlockSpec((chans, 1), lambda t: (0, 0)),
        pl.BlockSpec((chans, tall, 2 * MY), lambda t: (0, first + t, 0)),
        pl.BlockSpec(back_cols.shape, lambda t: (0, 0)),
        pl.BlockSpec(block, lambda t: (0, t, 0)),
        pl.BlockSpec(block, lambda t: (0, t, 0)),
    ]
    operands = [bias, rowback, back_cols, home, came]
    aliases = {}
    if held is not None:
        in_specs.append(pl.BlockSpec(memory_space=pl.ANY))
        operands.append(held)
        aliases = {5: 0}
    size = chans * rows * width
    return pl.pallas_call(
        final_kernel,
        grid=(rows // tall,),
        in_specs=in_specs,
        out_specs=pl.BlockSpec(block, lambda t: (0, first + t, 0)),
        out_shape=jax.ShapeDtypeStruct((chans, row_count, width), jnp.bfloat16),
        input_output_aliases=aliases,
        compiler_params=pltpu.CompilerParams(vmem_limit_bytes=48 << 20),
        cost_estimate=pl.CostEstimate(
            flops=2 * size * 2 * MY, bytes_accessed=3 * size * 2, transcendentals=size
        ),
    )(*operands)


def on_device(image, spec_weight, point_weight, bias):
    chan_count, row_count, width_len = image.shape
    row_index = lax.axis_index("row")
    row_devs = lax.axis_size("row")
    chan_devs = lax.axis_size("chan")
    chan_index = lax.axis_index("chan")
    full_rows = row_count * row_devs

    core_swap = [(c, c ^ 1) for c in range(chan_devs)]
    chip_swap = [(c, c ^ 2) for c in range(chan_devs)]
    chunks = chunk_rows(row_count)
    def swap(part, start, rows):
        mine = lax.slice_in_dim(part, start, start + rows, axis=1)
        return lax.ppermute(mine, "chan", core_swap)

    first_mine = lax.slice_in_dim(image, 0, chunks[0][1], axis=1)
    first_far = lax.ppermute(first_mine, "chan", chip_swap)
    first_mine, image = lax.optimization_barrier((first_mine, image))

    def kron(out_dev, in_dev):
        eye = jnp.eye(UNIT, dtype=jnp.bfloat16)
        blocks = [
            lax.dynamic_slice(
                point_weight, (out_dev * chan_count, dev * chan_count), (chan_count, chan_count)
            )
            for dev in (in_dev, in_dev ^ 1)
        ]
        small = jnp.concatenate(blocks, 1)
        large = small[:, None, :, None] * eye[None, :, None, :]
        return large.reshape(chan_count * UNIT, 2 * chan_count * UNIT)

    kron_home = kron(chan_index, chan_index)
    kron_far = kron(chan_index, chan_index ^ 2)
    kron_both = jnp.concatenate([kron(chan_index ^ 2, chan_index), kron_home], 0)

    cames = {}
    homes = {}
    done = []

    peers = {}

    def meet(n):
        if n < len(chunks):
            peers[n] = swap(image, *chunks[n])

    def issue(n):
        if n >= len(chunks):
            return
        peer = peers[n]
        away, homes[n] = partials(image, peer, kron_both, *chunks[n])
        before = 3 * (n - SLACK) + 4
        if n >= SLACK:
            finish_until(before)
            away, done[before - 1] = lax.optimization_barrier((away, done[before - 1]))
        cames[n] = lax.ppermute(away, "chan", chip_swap)

    def gate(n, *values):
        if n + 1 >= len(chunks):
            return values
        cames[n], homes[n + 1], *values = lax.optimization_barrier(
            (cames[n], homes[n + 1], *values)
        )
        return values

    def finish_until(count):
        while len(done) < count:
            n = len(done)
            last = done[-1] if done else None
            done.append(
                finish(bias, rowback, back_cols, homes[n], cames[n], chunks[n][0], last)
            )

    meet(1)
    meet(2)
    issue(1)
    issue(2)
    col_pts = jnp.arange(width_len, dtype=jnp.int32)
    row_global = row_index * row_count + jnp.arange(row_count, dtype=jnp.int32)
    bias = bias[:, None]
    first_far, first_mine, image, col_pts = gate(1, first_far, first_mine, image, col_pts)
    meet(3)
    meet(4)
    issue(3)
    image, row_global = gate(2, image, row_global)

    col_freq = jnp.arange(MY, dtype=jnp.int32)
    cos_w, sin_w = wave_table(col_pts, col_freq, width_len)
    fwd_cols = jnp.concatenate([cos_w, -sin_w], 1).astype(jnp.bfloat16)
    back_cols = jnp.concatenate([cos_w.T, -sin_w.T], 0).astype(jnp.bfloat16)
    back_cols = back_cols * jnp.bfloat16(1.0 / math.sqrt(MY))
    row_freq = jnp.arange(MX, dtype=jnp.int32) - MX // 2
    colspec = jnp.dot(
        image.reshape(chan_count * row_count, width_len),
        fwd_cols,
        preferred_element_type=jnp.float32,
    )
    colspec = (
        (colspec * (1.0 / math.sqrt(width_len)))
        .astype(jnp.bfloat16)
        .reshape(chan_count, row_count, 2 * MY)
    )
    meet(5)
    issue(4)
    image, colspec = gate(3, image, colspec)
    meet(6)
    issue(5)
    cos_h, sin_h = wave_table(row_global, row_freq, full_rows)
    fwd_rows = jnp.concatenate([cos_h, sin_h], 1).astype(jnp.bfloat16)
    partial_value = jnp.einsum("chp,hq->cqp", colspec, fwd_rows, preferred_element_type=jnp.float32)
    spec_re = partial_value[:, :MX, :MY] + partial_value[:, MX:, MY:]
    spec_im = partial_value[:, :MX, MY:] - partial_value[:, MX:, :MY]
    partial_value = jnp.concatenate([spec_re, spec_im], -1) * (1.0 / math.sqrt(full_rows))
    block = lax.psum_scatter(partial_value, "row", scatter_dimension=1, tiled=True)
    image, block = gate(4, image, block)
    meet(7)
    issue(6)
    spectrum = block.astype(jnp.bfloat16)
    all_inputs = lax.all_gather(spectrum, "chan", axis=0, tiled=True)
    zed_re = all_inputs[..., :MY].astype(jnp.float32)
    zed_im = all_inputs[..., MY:].astype(jnp.float32)
    wgt_re = spec_weight[0].astype(jnp.float32)
    wgt_im = spec_weight[1].astype(jnp.float32)
    mix_re = jnp.einsum("kiop,ikp->okp", wgt_re, zed_re) - jnp.einsum(
        "kiop,ikp->okp", wgt_im, zed_im
    )
    mix_im = jnp.einsum("kiop,ikp->okp", wgt_re, zed_im) + jnp.einsum(
        "kiop,ikp->okp", wgt_im, zed_re
    )
    mixed = jnp.concatenate([mix_re, mix_im], -1).astype(jnp.bfloat16)
    piece = lax.all_gather(mixed, "row", axis=1, tiled=True)
    image, piece = gate(5, image, piece)
    meet(8)
    issue(7)
    (image,) = gate(6, image)
    meet(9)
    issue(8)
    cos_back = cos_h.T.astype(jnp.bfloat16)
    sin_back = sin_h.T.astype(jnp.bfloat16)
    with_cos = jnp.einsum("okp,kh->ohp", piece, cos_back, preferred_element_type=jnp.float32)
    with_sin = jnp.einsum("okp,kh->ohp", piece, sin_back, preferred_element_type=jnp.float32)
    back_re = with_cos[..., :MY] - with_sin[..., MY:]
    back_im = with_sin[..., :MY] + with_cos[..., MY:]
    rowback = (jnp.concatenate([back_re, back_im], -1) * (1.0 / math.sqrt(MX))).astype(jnp.bfloat16)

    first_peer = lax.ppermute(first_mine, "chan", core_swap)
    (homes[0],) = partials(image, first_peer, kron_home, *chunks[0])
    first_other = lax.ppermute(first_far, "chan", core_swap)
    (cames[0],) = partials(first_far, first_other, kron_far, 0, chunks[0][1])
    for n in range(9, len(chunks)):
        (image,) = gate(n - 2, image)
        meet(n + 1)
        issue(n)
    finish_until(len(chunks))
    return done[-1]


def solution(mesh):
    in_specs = (P("chan", "row", None), P(None, "row", None, "chan", None), P(), P("chan"))
    out_specs = P("chan", "row", None)
    return jax.shard_map(
        on_device, mesh=mesh, in_specs=in_specs, out_specs=out_specs, check_vma=False
    )
```
